32 devices in a mesh: box: 16 (over z, y, core), tx: 2 (over x).
Axes of the slice: x: 2, y: 2, z: 4, core: 2. Of those that a mesh axis runs over, the one named last changes fastest.
Arguments:
- bank: bfloat16 [512, 512, 1024], P('box', 'tx'), may hold values from -6 to 6
- pick: int32 [32], replicated, may hold values from 0 to 511, as said below
- slot_box: int32 [512], replicated, may hold values from 0 to 511, each once
- leaf_factor: bfloat16 [512, 512, 128], P('box'), may hold values from -0.1875 to 0.1875
- self_factor: bfloat16 [9, 512, 64, 128], P(None, 'box'), may hold values from -0.375 to 0.375
- cross_factor: bfloat16 [9, 512, 64, 128], P(None, 'box'), may hold values from -0.375 to 0.375
- target_factor: bfloat16 [512, 64, 4096], P('box'), may hold values from -0.5 to 0.5
Outputs:
- field: bfloat16 [512, 32, 4096], P('box', 'tx')
The draws below stay inside these ranges and needn't reach their ends.
Inputs may be any that keep to these rules, and one draw needn't show every extreme that they name: `pick`: distinct stored transmitters. `slot_box`: each box once.
All inputs are finite; a program needn't handle non-finite values.
Results may differ from the reference program's by a relative error of at most 0.023.
Values may be sent and summed in bfloat16 or wider, within the bound.
No kernel may reach another device: no remote copies, remote signals or barrier semaphores. Data moves between devices by JAX's collectives and lax.ppermute only.
A program may use at most 128 MiB of HBM per device.

```python
import jax
import jax.numpy as jnp

NB = 512
LEVELS = 9
K = 64
UNK = 512
PTS = 2048
TXC = 32
BANK = 512


def draw_pick(key, part):
    first_key = jax.random.fold_in(key, 11)
    second_key = jax.random.fold_in(key, 12)
    middle = jax.random.permutation(first_key, BANK - 2)[:TXC - 2] + 1
    joined = jnp.concatenate([jnp.array([0, BANK - 1], dtype=jnp.int32), middle.astype(jnp.int32)])
    order = jax.random.permutation(second_key, TXC)
    return joined[order].astype(jnp.int32)


def block_scale(key, dims, cuts, low, largest):
    level, own = 1.0, jax.random.fold_in(key, 6)
    for dim, blocks in cuts:
        heights = jnp.exp(jax.random.uniform(jax.random.fold_in(own, dim), (blocks,), jnp.float32, low / len(cuts), largest / len(cuts)))
        level = level * jnp.repeat(heights, dims[dim] // blocks).reshape([-1 if axis == dim else 1 for axis in range(len(dims))])
    return level


def bell_draw(stream_key, extent, width, reach, cuts=(), kind=jnp.bfloat16):
    loudness = block_scale(stream_key, extent, cuts, -0.22, 0.18) if cuts else 1.0
    result = jax.random.normal(stream_key, extent, jnp.float32) * width * loudness
    return jnp.minimum(jnp.maximum(result, -reach), reach).astype(kind)


def setup_inputs(seed: int = 0) -> dict:
    key_of = jax.random.split(jax.random.key(seed), 8)
    bank = bell_draw(key_of[0], (NB, BANK, 2 * UNK), 1.0, 6.0, ((0, 16), (1, 2)))
    pick = draw_pick(jax.random.fold_in(key_of[7], 71), 0)
    slot_box = jax.random.permutation(key_of[2], NB).astype(jnp.int32)
    leaf_factor = bell_draw(key_of[3], (NB, UNK, 2 * K), (2 * UNK) ** -0.5, 0.1875, ((0, 16),))
    self_factor = bell_draw(key_of[4], (LEVELS, NB, K, 2 * K), (4 * K) ** -0.5, 0.375, ((1, 16),))
    cross_factor = bell_draw(key_of[5], (LEVELS, NB, K, 2 * K), (4 * K) ** -0.5, 0.375, ((1, 16),))
    target_factor = bell_draw(key_of[6], (NB, K, 2 * PTS), (2 * K) ** -0.5, 0.5, ((0, 16),))
    return dict(bank=bank, pick=pick, slot_box=slot_box, leaf_factor=leaf_factor, self_factor=self_factor, cross_factor=cross_factor, target_factor=target_factor)


def complex_times(values, matrix):
    inner = matrix.shape[-2]
    half = matrix.shape[-1] // 2
    mat = matrix.astype(jnp.float32)
    first = jnp.einsum("brn,bnk->brk", values[..., :inner].astype(jnp.float32), mat)
    second = jnp.einsum("brn,bnk->brk", values[..., inner:].astype(jnp.float32), mat)
    return jnp.concatenate([first[..., :half] - second[..., half:], first[..., half:] + second[..., :half]], axis=-1)


def reference(bank, pick, slot_box, leaf_factor, self_factor, cross_factor, target_factor):
    selected = jnp.take(bank, pick, axis=1)
    coefs = complex_times(selected, leaf_factor).astype(jnp.bfloat16)
    current = jnp.take(coefs, slot_box, axis=0)
    slots = jnp.arange(NB, dtype=jnp.int32)
    for level in range(LEVELS):
        partner = jnp.take(current, jnp.bitwise_xor(slots, 1 << level), axis=0)
        mixed = complex_times(current, self_factor[level]) + complex_times(partner, cross_factor[level])
        current = mixed.astype(jnp.bfloat16)
    return complex_times(current, target_factor).astype(jnp.bfloat16)
```

```python
import functools

import jax
import jax.numpy as jnp
from jax import lax
from jax.experimental import pallas as pl
from jax.experimental.pallas import tpu as pltpu
from jax.sharding import PartitionSpec as P

BF16 = jnp.bfloat16
F32 = jnp.float32
MIB = 1 << 20
BATCH = 4


def dot(a, b):
    return jnp.dot(a, b, preferred_element_type=F32)


def lanes_below(shape, bound):
    return lax.broadcasted_iota(jnp.int32, shape, len(shape) - 1) < bound


def combine(first, second, rank):
    turned = pltpu.roll(second, rank, 1)
    return first + jnp.where(lanes_below(turned.shape, rank), -turned, turned)


def stack_pair(own, other, rank):
    low = lanes_below(own.shape, rank)
    real = jnp.where(low, own, pltpu.roll(other, rank, 1))
    imag = jnp.where(low, pltpu.roll(own, rank, 1), other)
    return jnp.concatenate([real, imag], axis=0).astype(BF16)


def leaf_kernel(
    cols,
    pick_ref,
    slot_ref,
    bank_ref,
    leaf_ref,
    out_ref,
    perm_ref,
    bank,
    leaf,
    chooser,
    chosen,
    coefs,
    bank_sems,
    leaf_sems,
):
    box_dev, stored, unknowns = bank_ref.shape
    unknowns //= 2
    rank = leaf_ref.shape[-1] // 2
    picked = pick_ref.shape[0]

    def bank_copy(b):
        return pltpu.make_async_copy(bank_ref.at[b], bank.at[b], bank_sems.at[b])

    def leaf_copy(b):
        return pltpu.make_async_copy(leaf_ref.at[b], leaf.at[b], leaf_sems.at[b])

    def start(b, _):
        bank_copy(b).start()
        leaf_copy(b).start()
        return 0

    lax.fori_loop(0, box_dev, start, 0)

    base = lax.axis_index("tx") * stored
    row = lax.broadcasted_iota(jnp.int32, (picked, stored), 0)
    column = lax.broadcasted_iota(jnp.int32, (picked, stored), 1)
    wanted = jnp.full((picked, stored), -1, jnp.int32)
    for c in range(picked):
        wanted = jnp.where(row == c, pick_ref[c] - base, wanted)
    chooser[...] = (wanted == column).astype(F32).astype(BF16)
    count = slot_ref.shape[1]
    for c in range(0, count, 128):
        box = lax.broadcasted_iota(jnp.int32, (count, 128), 0)
        hit = (box == slot_ref[:, c : c + 128]).astype(F32)
        perm_ref[c : c + 128, :] = hit.T.astype(BF16)

    def select(g):
        for i in range(BATCH):
            bank_copy(g * BATCH + i).wait()
        for i in range(BATCH):
            rows = dot(chooser[...], bank[g * BATCH + i]).astype(BF16)
            chosen[g % 2, i] = jnp.concatenate([rows[:, :unknowns], rows[:, unknowns:]], axis=0)

    def map_leaves(g):
        for i in range(BATCH):
            leaf_copy(g * BATCH + i).wait()
        for i in range(BATCH):
            product = dot(chosen[g % 2, i], leaf[g * BATCH + i])
            place = pl.multiple_of((g * BATCH + i) * picked, picked)
            coefs[pl.ds(place, picked), :] = combine(product[:picked], product[picked:], rank)

    def advance(g, _):
        for i in range(BATCH):
            bank_copy(g * BATCH + i).wait()
            leaf_copy((g - 1) * BATCH + i).wait()
        for i in range(BATCH):
            rows = dot(chooser[...], bank[g * BATCH + i]).astype(BF16)
            chosen[g % 2, i] = jnp.concatenate([rows[:, :unknowns], rows[:, unknowns:]], axis=0)
            product = dot(chosen[(g - 1) % 2, i], leaf[(g - 1) * BATCH + i])
            place = pl.multiple_of(((g - 1) * BATCH + i) * picked, picked)
            coefs[pl.ds(place, picked), :] = combine(product[:picked], product[picked:], rank)
        return 0

    batches = box_dev // BATCH
    select(0)
    lax.fori_loop(1, batches, advance, 0)
    map_leaves(batches - 1)
    groups = picked // cols
    for c in range(picked):
        place = (c % cols) * groups + c // cols
        out_ref[place] = coefs[pl.ds(c, box_dev, stride=picked), :].astype(BF16)


def leaf_step(cols, bank, pick, slot_box, leaf_factor):
    box_dev, stored, width = bank.shape
    picked = pick.shape[0]
    count = slot_box.shape[0]
    rank2 = leaf_factor.shape[-1]
    return pl.pallas_call(
        functools.partial(leaf_kernel, cols),
        out_shape=(
            jax.ShapeDtypeStruct((picked, box_dev, rank2), BF16),
            jax.ShapeDtypeStruct((count, count), BF16),
        ),
        in_specs=[
            pl.BlockSpec(memory_space=pltpu.SMEM),
            pl.BlockSpec(memory_space=pltpu.VMEM),
            pl.BlockSpec(memory_space=pltpu.HBM),
            pl.BlockSpec(memory_space=pltpu.HBM),
        ],
        out_specs=(
            pl.BlockSpec(memory_space=pltpu.VMEM),
            pl.BlockSpec(memory_space=pltpu.VMEM),
        ),
        scratch_shapes=[
            pltpu.VMEM(bank.shape, BF16),
            pltpu.VMEM(leaf_factor.shape, BF16),
            pltpu.VMEM((picked, stored), BF16),
            pltpu.VMEM((2, BATCH, 2 * picked, width // 2), BF16),
            pltpu.VMEM((box_dev * picked, rank2), F32),
            pltpu.SemaphoreType.DMA((box_dev,)),
            pltpu.SemaphoreType.DMA((box_dev,)),
        ],
        compiler_params=pltpu.CompilerParams(vmem_limit_bytes=56 * MIB),
        name="select_and_leaf",
    )(pick, slot_box.reshape(1, count), bank, leaf_factor)


def order_kernel(perm_ref, sent_ref, out_ref):
    devices, groups, box_dev, width = sent_ref.shape
    total = sent_ref[:, 0].astype(F32)
    for t in range(1, groups):
        total = total + sent_ref[:, t].astype(F32)
    rows = total.reshape(devices * box_dev, width).astype(BF16)
    out_ref[...] = dot(perm_ref[...], rows).astype(BF16).reshape(out_ref.shape)


def order_step(perm, sent):
    devices, _, box_dev, width = sent.shape
    return pl.pallas_call(
        order_kernel,
        out_shape=jax.ShapeDtypeStruct((devices, box_dev, width), BF16),
        in_specs=[pl.BlockSpec(memory_space=pltpu.VMEM)] * 2,
        out_specs=pl.BlockSpec(memory_space=pltpu.VMEM),
        compiler_params=pltpu.CompilerParams(vmem_limit_bytes=8 * MIB),
        name="leaf_order",
    )(perm, sent)


def local_kernel(local_bits, leaves_ref, self_ref, cross_ref, out_ref, wide, state):
    cols, slots, rank2 = leaves_ref.shape
    rank = rank2 // 2
    wide[...] = leaves_ref[...].astype(F32).reshape(cols * slots, rank2)
    for s in range(slots):
        state[0, s] = wide[pl.ds(s, cols, stride=slots), :]
    for level in range(local_bits):
        span = 1 << level
        now, later = level % 2, (level + 1) % 2
        for s in range(slots):
            if s & span:
                continue
            p = s | span
            left = jnp.concatenate([self_ref[level, s], cross_ref[level, s]], axis=0)
            right = jnp.concatenate([cross_ref[level, p], self_ref[level, p]], axis=0)
            both = dot(
                stack_pair(state[now, s], state[now, p], rank),
                jnp.concatenate([left, right], axis=1),
            )
            for place, product in ((s, both[:, :rank2]), (p, both[:, rank2:])):
                mixed = combine(product[:cols], product[cols:], rank)
                if level == local_bits - 1:
                    out_ref[place] = mixed.astype(BF16)
                else:
                    state[later, place] = mixed


def local_step(local_bits, leaves, self_factor, cross_factor):
    cols, slots, rank2 = leaves.shape
    return pl.pallas_call(
        functools.partial(local_kernel, local_bits),
        out_shape=jax.ShapeDtypeStruct((slots, cols, rank2), BF16),
        in_specs=[pl.BlockSpec(memory_space=pltpu.VMEM)] * 3,
        out_specs=pl.BlockSpec(memory_space=pltpu.VMEM),
        scratch_shapes=[
            pltpu.VMEM((cols * slots, rank2), F32),
            pltpu.VMEM((2, slots, cols, rank2), F32),
        ],
        compiler_params=pltpu.CompilerParams(vmem_limit_bytes=16 * MIB),
        name="local_levels",
    )(leaves, self_factor, cross_factor)


def mix_slot(level, s, own_ref, other_ref, self_ref, cross_ref):
    cols, rank2 = own_ref.shape[1:]
    rank = rank2 // 2
    rows = stack_pair(own_ref[s].astype(F32), other_ref[s].astype(F32), rank)
    product = dot(rows, jnp.concatenate([self_ref[level, s], cross_ref[level, s]], axis=0))
    return combine(product[:cols], product[cols:], rank)


def pair_kernel(level, own_ref, other_ref, self_ref, cross_ref, out_ref):
    for s in range(own_ref.shape[0]):
        out_ref[s] = mix_slot(level, s, own_ref, other_ref, self_ref, cross_ref).astype(BF16)


def pair_step(level, own, other, self_factor, cross_factor):
    return pl.pallas_call(
        functools.partial(pair_kernel, level),
        out_shape=jax.ShapeDtypeStruct(own.shape, BF16),
        in_specs=[pl.BlockSpec(memory_space=pltpu.VMEM)] * 4,
        out_specs=pl.BlockSpec(memory_space=pltpu.VMEM),
        compiler_params=pltpu.CompilerParams(vmem_limit_bytes=16 * MIB),
        name="pair_level",
    )(own, other, self_factor, cross_factor)


GROUP = 4
TILE = 512


def field_kernel(
    level, own_ref, other_ref, self_ref, cross_ref, target_ref, out_ref, final, result, sems
):
    slots, cols, rank2 = own_ref.shape
    rank = rank2 // 2
    points = target_ref.shape[-1] // 2
    for s in range(slots):
        final[s] = mix_slot(level, s, own_ref, other_ref, self_ref, cross_ref)

    def out_copy(q):
        part = pl.ds(q * GROUP, GROUP)
        return pltpu.make_async_copy(result.at[part], out_ref.at[part], sems.at[q])

    def group(q, _):
        rows = []
        for i in range(GROUP):
            values = final[q * GROUP + i]
            turned = pltpu.roll(values, rank, 1)
            low = lanes_below(values.shape, rank)
            real, imag = (values, turned) if i % 2 == 0 else (turned, values)
            keep = low if i % 2 == 0 else jnp.logical_not(low)
            block = jnp.concatenate([jnp.where(keep, real, 0.0), jnp.where(keep, imag, 0.0)], axis=0)
            empty = jnp.zeros_like(block)
            rows.append(
                jnp.concatenate([block if j == i // 2 else empty for j in range(GROUP // 2)], axis=1)
            )
        rows = jnp.concatenate(rows, axis=0).astype(BF16)
        part = pl.ds(q * GROUP, GROUP)
        for start in range(0, points, TILE):
            real_part = target_ref[part, :, pl.ds(start, TILE)].reshape(GROUP * rank, TILE)
            imag_part = target_ref[part, :, pl.ds(points + start, TILE)].reshape(GROUP * rank, TILE)
            by_real = dot(rows, real_part)
            by_imag = dot(rows, imag_part)
            for i in range(GROUP):
                xr = slice(2 * cols * i, 2 * cols * i + cols)
                xi = slice(2 * cols * i + cols, 2 * cols * (i + 1))
                box = q * GROUP + i
                result[box, :, pl.ds(start, TILE)] = (by_real[xr] - by_imag[xi]).astype(BF16)
                result[box, :, pl.ds(points + start, TILE)] = (by_imag[xr] + by_real[xi]).astype(BF16)
        out_copy(q).start()
        return 0

    lax.fori_loop(0, slots // GROUP, group, 0)
    for q in range(slots // GROUP):
        out_copy(q).wait()


def field_step(level, own, other, self_factor, cross_factor, target_factor):
    slots, cols, rank2 = own.shape
    width = target_factor.shape[-1]
    return pl.pallas_call(
        functools.partial(field_kernel, level),
        out_shape=jax.ShapeDtypeStruct((slots, cols, width), BF16),
        in_specs=[pl.BlockSpec(memory_space=pltpu.VMEM)] * 5,
        out_specs=pl.BlockSpec(memory_space=pl.ANY),
        scratch_shapes=[
            pltpu.VMEM((slots, cols, rank2), F32),
            pltpu.VMEM((slots, cols, width), BF16),
            pltpu.SemaphoreType.DMA((slots // GROUP,)),
        ],
        compiler_params=pltpu.CompilerParams(vmem_limit_bytes=22 * MIB),
        name="last_level_and_field",
    )(own, other, self_factor, cross_factor, target_factor)


def per_device(bank, pick, slot_box, leaf_factor, self_factor, cross_factor, target_factor):
    box_dev = bank.shape[0]
    devices = lax.axis_size("box")
    groups = lax.axis_size("tx")
    cols = pick.shape[0] // groups
    rank2 = leaf_factor.shape[-1]
    levels = self_factor.shape[0]
    local_bits = box_dev.bit_length() - 1
    parts = devices // cols
    width = rank2 // parts

    sent, perm = leaf_step(cols, bank, pick, slot_box, leaf_factor)
    if parts > 1:
        sent = sent.reshape(cols, groups, box_dev, parts, width).transpose(0, 3, 1, 2, 4)
        sent = sent.reshape(devices * groups, box_dev, width)
    sent = lax.all_to_all(sent, ("box", "tx"), 0, 0, tiled=True)
    ordered = order_step(perm, sent.reshape(devices, groups, box_dev, width))
    leaves = lax.all_to_all(ordered, "box", 0, 0, tiled=True)
    if parts > 1:
        leaves = leaves.reshape(cols, parts, box_dev, width).transpose(0, 2, 1, 3)
        leaves = leaves.reshape(cols, box_dev, rank2)
    current = local_step(local_bits, leaves, self_factor, cross_factor)
    for level in range(local_bits, levels):
        bit = 1 << (level - local_bits)
        other = lax.ppermute(current, "box", [(i, i ^ bit) for i in range(devices)])
        if level < levels - 1:
            current = pair_step(level, current, other, self_factor, cross_factor)
    return field_step(level, current, other, self_factor, cross_factor, target_factor)


def solution(mesh):
    in_specs = (
        P("box", "tx", None),
        P(),
        P(),
        P("box", None, None),
        P(None, "box", None, None),
        P(None, "box", None, None),
        P("box", None, None),
    )
    out_specs = P("box", "tx", None)
    return jax.shard_map(
        per_device, mesh=mesh, in_specs=in_specs, out_specs=out_specs, check_vma=False
    )
```

```python
import functools

import jax
import jax.numpy as jnp
from jax import lax
from jax.experimental import pallas as pl
from jax.experimental.pallas import tpu as pltpu
from jax.sharding import PartitionSpec as P

BF16 = jnp.bfloat16
F32 = jnp.float32
MIB = 1 << 20
BATCH = 8
UNROLL = 8
ROWS = 16
LEAF_VMEM = 48


def dot(a, b):
    return jnp.dot(a, b, preferred_element_type=F32)


def lanes_below(shape, bound):
    return lax.broadcasted_iota(jnp.int32, shape, len(shape) - 1) < bound


def combine(first, second, rank):
    turned = pltpu.roll(second, rank, 1)
    return first + jnp.where(lanes_below(turned.shape, rank), -turned, turned)


def stack_pair(own, other, rank):
    low = lanes_below(own.shape, rank)
    real = jnp.where(low, own, pltpu.roll(other, rank, 1))
    imag = jnp.where(low, pltpu.roll(own, rank, 1), other)
    return jnp.concatenate([real, imag], axis=0).astype(BF16)


def leaf_kernel(
    cols,
    pick_hbm,
    slot_hbm,
    bank_ref,
    leaf_ref,
    out_ref,
    perm_ref,
    pick_ref,
    slot_ref,
    bank,
    leaf,
    coefs,
    present,
    wanted,
    rank_of,
    index_sems,
    bank_sems,
    leaf_sems,
):
    box_dev, stored, unknowns = bank_ref.shape
    unknowns //= 2
    rank = leaf_ref.shape[-1] // 2
    picked = pick_ref.shape[0]
    base = lax.axis_index("tx") * stored
    batches = box_dev // BATCH
    row_groups = stored // ROWS

    def leaf_copy(g):
        part = pl.ds(g * BATCH, BATCH)
        return pltpu.make_async_copy(leaf_ref.at[part], leaf.at[part], leaf_sems.at[g])

    def bank_copy(g, j):
        part = pl.ds(g * BATCH, BATCH)
        source = pl.ds(pl.multiple_of(wanted[j] * ROWS, ROWS), ROWS)
        target = pl.ds(pl.multiple_of(j * ROWS, ROWS), ROWS)
        return pltpu.make_async_copy(
            bank_ref.at[part, source], bank.at[part, target], bank_sems.at[g, j]
        )

    pick_copy = pltpu.make_async_copy(pick_hbm, pick_ref, index_sems.at[0])
    slot_copy = pltpu.make_async_copy(slot_hbm, slot_ref, index_sems.at[1])
    pick_copy.start()
    slot_copy.start()
    leaf_copy(0).start()
    pick_copy.wait()
    for k in range(row_groups):
        present[k] = 0
    for c in range(picked):
        place = pick_ref[c] - base

        @pl.when(jnp.logical_and(place >= 0, place < stored))
        def _():
            present[place // ROWS] = 1

    count = jnp.int32(0)
    for k in range(row_groups):
        wanted[count] = k
        rank_of[k] = count
        count = count + present[k]

    def start(g, _):
        lax.fori_loop(0, count, lambda j, _: (bank_copy(g, j).start(), 0)[1], 0)

        @pl.when(g > 0)
        def _():
            leaf_copy(g).start()

        return 0

    lax.fori_loop(0, batches, start, 0)

    slot_copy.wait()
    boxes = slot_ref.shape[1]
    for c in range(0, boxes, 128):
        box = lax.broadcasted_iota(jnp.int32, (boxes, 128), 0)
        hit = (box == slot_ref[:, c : c + 128]).astype(F32)
        perm_ref[c : c + 128, :] = hit.T.astype(BF16)

    def map_batch(g, _):
        leaf_copy(g).wait()
        lax.fori_loop(0, count, lambda j, _: (bank_copy(g, j).wait(), 0)[1], 0)

        def map_boxes(rows):
            def step(k, _):
                for i in range(UNROLL):
                    b = g * BATCH + k * UNROLL + i
                    first = dot(bank[b, :rows, :unknowns], leaf[b])
                    second = dot(bank[b, :rows, unknowns:], leaf[b])
                    place = pl.ds(pl.multiple_of(b * stored, stored), rows)
                    coefs[place, :] = combine(first, second, rank)
                return 0

            lax.fori_loop(0, BATCH // UNROLL, step, 0)

        quarter = row_groups // 4
        for part in range(2, 5):
            low = 0 if part == 2 else (part - 1) * quarter
            fits = jnp.logical_and(count > low, count <= part * quarter)
            pl.when(fits)(functools.partial(map_boxes, part * quarter * ROWS))
        return 0

    lax.fori_loop(0, batches, map_batch, 0)
    groups = picked // cols
    for c in range(picked):
        place = pick_ref[c] - base
        held = jnp.logical_and(place >= 0, place < stored)
        place = jnp.where(held, place, 0)
        row = jnp.where(held, rank_of[place // ROWS] * ROWS + place % ROWS, 0)
        rows = coefs[pl.ds(row, box_dev, stride=stored), :]
        out_ref[(c % cols) * groups + c // cols] = jnp.where(held, rows, 0.0).astype(BF16)


def leaf_step(cols, bank, pick, slot_box, leaf_factor):
    box_dev, stored, _ = bank.shape
    picked = pick.shape[0]
    boxes = slot_box.shape[0]
    rank2 = leaf_factor.shape[-1]
    return pl.pallas_call(
        functools.partial(leaf_kernel, cols),
        out_shape=(
            jax.ShapeDtypeStruct((picked, box_dev, rank2), BF16),
            jax.ShapeDtypeStruct((boxes, boxes), BF16),
        ),
        in_specs=[
            pl.BlockSpec(memory_space=pltpu.HBM),
            pl.BlockSpec(memory_space=pltpu.HBM),
            pl.BlockSpec(memory_space=pltpu.HBM),
            pl.BlockSpec(memory_space=pltpu.HBM),
        ],
        out_specs=(
            pl.BlockSpec(memory_space=pltpu.VMEM),
            pl.BlockSpec(memory_space=pltpu.VMEM),
        ),
        scratch_shapes=[
            pltpu.SMEM(pick.shape, jnp.int32),
            pltpu.VMEM((1, boxes), jnp.int32),
            pltpu.VMEM(bank.shape, BF16),
            pltpu.VMEM(leaf_factor.shape, BF16),
            pltpu.VMEM((box_dev * stored, rank2), F32),
            pltpu.SMEM((stored // ROWS,), jnp.int32),
            pltpu.SMEM((stored // ROWS,), jnp.int32),
            pltpu.SMEM((stored // ROWS,), jnp.int32),
            pltpu.SemaphoreType.DMA((2,)),
            pltpu.SemaphoreType.DMA((box_dev // BATCH, stored // ROWS)),
            pltpu.SemaphoreType.DMA((box_dev // BATCH,)),
        ],
        compiler_params=pltpu.CompilerParams(vmem_limit_bytes=LEAF_VMEM * MIB),
        name="select_and_leaf",
    )(
        pltpu.with_memory_space_constraint(pick, pltpu.HBM),
        pltpu.with_memory_space_constraint(slot_box.reshape(1, boxes), pltpu.HBM),
        pltpu.with_memory_space_constraint(bank, pltpu.HBM),
        pltpu.with_memory_space_constraint(leaf_factor, pltpu.HBM),
    )


def order_kernel(perm_ref, sent_ref, out_ref):
    devices, groups, box_dev, width = sent_ref.shape
    total = sent_ref[:, 0].astype(F32)
    for t in range(1, groups):
        total = total + sent_ref[:, t].astype(F32)
    rows = total.reshape(devices * box_dev, width).astype(BF16)
    out_ref[...] = dot(perm_ref[...], rows).astype(BF16).reshape(out_ref.shape)


def order_step(perm, sent):
    devices, _, box_dev, width = sent.shape
    return pl.pallas_call(
        order_kernel,
        out_shape=jax.ShapeDtypeStruct((devices, box_dev, width), BF16),
        in_specs=[pl.BlockSpec(memory_space=pltpu.VMEM)] * 2,
        out_specs=pl.BlockSpec(memory_space=pltpu.VMEM),
        compiler_params=pltpu.CompilerParams(vmem_limit_bytes=8 * MIB),
        name="leaf_order",
    )(perm, sent)


def local_kernel(local_bits, leaves_ref, self_ref, cross_ref, out_ref, wide, state):
    cols, slots, rank2 = leaves_ref.shape
    rank = rank2 // 2
    wide[...] = leaves_ref[...].astype(F32).reshape(cols * slots, rank2)
    for s in range(slots):
        state[0, s] = wide[pl.ds(s, cols, stride=slots), :]
    for level in range(local_bits):
        span = 1 << level
        now, later = level % 2, (level + 1) % 2
        for s in range(slots):
            if s & span:
                continue
            p = s | span
            left = jnp.concatenate([self_ref[level, s], cross_ref[level, s]], axis=0)
            right = jnp.concatenate([cross_ref[level, p], self_ref[level, p]], axis=0)
            both = dot(
                stack_pair(state[now, s], state[now, p], rank),
                jnp.concatenate([left, right], axis=1),
            )
            for place, product in ((s, both[:, :rank2]), (p, both[:, rank2:])):
                mixed = combine(product[:cols], product[cols:], rank)
                if level == local_bits - 1:
                    out_ref[place] = mixed.astype(BF16)
                else:
                    state[later, place] = mixed


def local_step(local_bits, leaves, self_factor, cross_factor):
    cols, slots, rank2 = leaves.shape
    return pl.pallas_call(
        functools.partial(local_kernel, local_bits),
        out_shape=jax.ShapeDtypeStruct((slots, cols, rank2), BF16),
        in_specs=[pl.BlockSpec(memory_space=pltpu.VMEM)] * 3,
        out_specs=pl.BlockSpec(memory_space=pltpu.VMEM),
        scratch_shapes=[
            pltpu.VMEM((cols * slots, rank2), F32),
            pltpu.VMEM((2, slots, cols, rank2), F32),
        ],
        compiler_params=pltpu.CompilerParams(vmem_limit_bytes=16 * MIB),
        name="local_levels",
    )(leaves, self_factor, cross_factor)


def mix_slot(level, s, own_ref, other_ref, self_ref, cross_ref):
    cols, rank2 = own_ref.shape[1:]
    rank = rank2 // 2
    rows = stack_pair(own_ref[s].astype(F32), other_ref[s].astype(F32), rank)
    product = dot(rows, jnp.concatenate([self_ref[level, s], cross_ref[level, s]], axis=0))
    return combine(product[:cols], product[cols:], rank)


def pair_kernel(level, own_ref, other_ref, self_ref, cross_ref, out_ref):
    for s in range(own_ref.shape[0]):
        out_ref[s] = mix_slot(level, s, own_ref, other_ref, self_ref, cross_ref).astype(BF16)


def pair_step(level, own, other, self_factor, cross_factor):
    return pl.pallas_call(
        functools.partial(pair_kernel, level),
        out_shape=jax.ShapeDtypeStruct(own.shape, BF16),
        in_specs=[pl.BlockSpec(memory_space=pltpu.VMEM)] * 4,
        out_specs=pl.BlockSpec(memory_space=pltpu.VMEM),
        compiler_params=pltpu.CompilerParams(vmem_limit_bytes=16 * MIB),
        name="pair_level",
    )(own, other, self_factor, cross_factor)


GROUP = 4
TILE = 512


def field_kernel(
    level, own_ref, other_ref, self_ref, cross_ref, target_ref, out_ref, final, result, sems
):
    slots, cols, rank2 = own_ref.shape
    rank = rank2 // 2
    points = target_ref.shape[-1] // 2
    for s in range(slots):
        final[s] = mix_slot(level, s, own_ref, other_ref, self_ref, cross_ref)

    def out_copy(q):
        part = pl.ds(q * GROUP, GROUP)
        return pltpu.make_async_copy(result.at[part], out_ref.at[part], sems.at[q])

    def group(q):
        rows = []
        for i in range(GROUP):
            values = final[q * GROUP + i]
            turned = pltpu.roll(values, rank, 1)
            low = lanes_below(values.shape, rank)
            real, imag = (values, turned) if i % 2 == 0 else (turned, values)
            keep = low if i % 2 == 0 else jnp.logical_not(low)
            block = jnp.concatenate([jnp.where(keep, real, 0.0), jnp.where(keep, imag, 0.0)], axis=0)
            empty = jnp.zeros_like(block)
            rows.append(
                jnp.concatenate([block if j == i // 2 else empty for j in range(GROUP // 2)], axis=1)
            )
        rows = jnp.concatenate(rows, axis=0).astype(BF16)
        part = pl.ds(q * GROUP, GROUP)
        for start in range(0, points, TILE):
            real_part = target_ref[part, :, pl.ds(start, TILE)].reshape(GROUP * rank, TILE)
            imag_part = target_ref[part, :, pl.ds(points + start, TILE)].reshape(GROUP * rank, TILE)
            by_real = dot(rows, real_part)
            by_imag = dot(rows, imag_part)
            for i in range(GROUP):
                xr = slice(2 * cols * i, 2 * cols * i + cols)
                xi = slice(2 * cols * i + cols, 2 * cols * (i + 1))
                box = q * GROUP + i
                result[box, :, pl.ds(start, TILE)] = (by_real[xr] - by_imag[xi]).astype(BF16)
                result[box, :, pl.ds(points + start, TILE)] = (by_imag[xr] + by_real[xi]).astype(BF16)
        out_copy(q).start()

    for q in range(slots // GROUP):
        group(q)
    for q in range(slots // GROUP):
        out_copy(q).wait()


def field_step(level, own, other, self_factor, cross_factor, target_factor):
    slots, cols, rank2 = own.shape
    width = target_factor.shape[-1]
    return pl.pallas_call(
        functools.partial(field_kernel, level),
        out_shape=jax.ShapeDtypeStruct((slots, cols, width), BF16),
        in_specs=[pl.BlockSpec(memory_space=pltpu.VMEM)] * 5,
        out_specs=pl.BlockSpec(memory_space=pl.ANY),
        scratch_shapes=[
            pltpu.VMEM((slots, cols, rank2), F32),
            pltpu.VMEM((slots, cols, width), BF16),
            pltpu.SemaphoreType.DMA((slots // GROUP,)),
        ],
        compiler_params=pltpu.CompilerParams(vmem_limit_bytes=22 * MIB),
        name="last_level_and_field",
    )(
        own,
        other,
        self_factor,
        cross_factor,
        pltpu.with_memory_space_constraint(target_factor, pltpu.VMEM),
    )


def per_device(bank, pick, slot_box, leaf_factor, self_factor, cross_factor, target_factor):
    box_dev = bank.shape[0]
    devices = lax.axis_size("box")
    groups = lax.axis_size("tx")
    cols = pick.shape[0] // groups
    rank2 = leaf_factor.shape[-1]
    levels = self_factor.shape[0]
    local_bits = box_dev.bit_length() - 1
    parts = devices // cols
    width = rank2 // parts

    sent, perm = leaf_step(cols, bank, pick, slot_box, leaf_factor)
    if parts > 1:
        sent = sent.reshape(cols, groups, box_dev, parts, width).transpose(0, 3, 1, 2, 4)
        sent = sent.reshape(devices * groups, box_dev, width)
    sent = lax.all_to_all(sent, ("box", "tx"), 0, 0, tiled=True)
    ordered = order_step(perm, sent.reshape(devices, groups, box_dev, width))
    leaves = lax.all_to_all(ordered, "box", 0, 0, tiled=True)
    if parts > 1:
        leaves = leaves.reshape(cols, parts, box_dev, width).transpose(0, 2, 1, 3)
        leaves = leaves.reshape(cols, box_dev, rank2)
    current = local_step(local_bits, leaves, self_factor, cross_factor)
    for level in range(local_bits, levels):
        bit = 1 << (level - local_bits)
        other = lax.ppermute(current, "box", [(i, i ^ bit) for i in range(devices)])
        if level < levels - 1:
            current = pair_step(level, current, other, self_factor, cross_factor)
    return field_step(level, current, other, self_factor, cross_factor, target_factor)


def solution(mesh):
    in_specs = (
        P("box", "tx", None),
        P(),
        P(),
        P("box", None, None),
        P(None, "box", None, None),
        P(None, "box", None, None),
        P("box", None, None),
    )
    out_specs = P("box", "tx", None)
    return jax.shard_map(
        per_device, mesh=mesh, in_specs=in_specs, out_specs=out_specs, check_vma=False
    )
```

```python
import functools

import jax
import jax.numpy as jnp
from jax import lax
from jax.experimental import pallas as pl
from jax.experimental.pallas import tpu as pltpu
from jax.sharding import PartitionSpec as P

BF16 = jnp.bfloat16
F32 = jnp.float32
MIB = 1 << 20
BATCH = 8
UNROLL = 8
ROWS = 16
LEAF_VMEM = 48
LAST_PARTS = 1


def dot(a, b):
    return jnp.dot(a, b, preferred_element_type=F32)


def lanes_below(shape, bound):
    return lax.broadcasted_iota(jnp.int32, shape, len(shape) - 1) < bound


def combine(first, second, rank):
    turned = pltpu.roll(second, rank, 1)
    return first + jnp.where(lanes_below(turned.shape, rank), -turned, turned)


def stack_pair(own, other, rank):
    low = lanes_below(own.shape, rank)
    real = jnp.where(low, own, pltpu.roll(other, rank, 1))
    imag = jnp.where(low, pltpu.roll(own, rank, 1), other)
    return jnp.concatenate([real, imag], axis=0).astype(BF16)


def leaf_kernel(
    cols,
    pick_hbm,
    slot_hbm,
    bank_ref,
    leaf_ref,
    out_ref,
    perm_ref,
    pick_ref,
    slot_ref,
    bank,
    leaf,
    coefs,
    present,
    wanted,
    rank_of,
    index_sems,
    bank_sems,
    leaf_sems,
):
    box_dev, stored, unknowns = bank_ref.shape
    unknowns //= 2
    rank = leaf_ref.shape[-1] // 2
    picked = pick_ref.shape[0]
    base = lax.axis_index("tx") * stored
    batches = box_dev // BATCH
    row_groups = stored // ROWS

    def leaf_copy(g):
        part = pl.ds(g * BATCH, BATCH)
        return pltpu.make_async_copy(leaf_ref.at[part], leaf.at[part], leaf_sems.at[g])

    def bank_copy(g, j):
        part = pl.ds(g * BATCH, BATCH)
        source = pl.ds(pl.multiple_of(wanted[j] * ROWS, ROWS), ROWS)
        target = pl.ds(pl.multiple_of(j * ROWS, ROWS), ROWS)
        return pltpu.make_async_copy(
            bank_ref.at[part, source], bank.at[part, target], bank_sems.at[g, j]
        )

    pick_copy = pltpu.make_async_copy(pick_hbm, pick_ref, index_sems.at[0])
    slot_copy = pltpu.make_async_copy(slot_hbm, slot_ref, index_sems.at[1])
    pick_copy.start()
    slot_copy.start()
    leaf_copy(0).start()
    pick_copy.wait()
    for k in range(row_groups):
        present[k] = 0
    for c in range(picked):
        place = pick_ref[c] - base

        @pl.when(jnp.logical_and(place >= 0, place < stored))
        def _():
            present[place // ROWS] = 1

    count = jnp.int32(0)
    for k in range(row_groups):
        wanted[count] = k
        rank_of[k] = count
        count = count + present[k]

    def start(g, _):
        lax.fori_loop(0, count, lambda j, _: (bank_copy(g, j).start(), 0)[1], 0)

        @pl.when(g > 0)
        def _():
            leaf_copy(g).start()

        return 0

    lax.fori_loop(0, batches, start, 0)

    slot_copy.wait()
    boxes = slot_ref.shape[1]
    for c in range(0, boxes, 128):
        box = lax.broadcasted_iota(jnp.int32, (boxes, 128), 0)
        hit = (box == slot_ref[:, c : c + 128]).astype(F32)
        perm_ref[c : c + 128, :] = hit.T.astype(BF16)

    def map_batch(g, _):
        leaf_copy(g).wait()
        lax.fori_loop(0, count, lambda j, _: (bank_copy(g, j).wait(), 0)[1], 0)

        def map_boxes(rows):
            def step(k, _):
                for i in range(UNROLL):
                    b = g * BATCH + k * UNROLL + i
                    first = dot(bank[b, :rows, :unknowns], leaf[b])
                    second = dot(bank[b, :rows, unknowns:], leaf[b])
                    place = pl.ds(pl.multiple_of(b * stored, stored), rows)
                    coefs[place, :] = combine(first, second, rank)
                return 0

            lax.fori_loop(0, BATCH // UNROLL, step, 0)

        quarter = row_groups // 4
        for part in range(2, 5):
            low = 0 if part == 2 else (part - 1) * quarter
            fits = jnp.logical_and(count > low, count <= part * quarter)
            pl.when(fits)(functools.partial(map_boxes, part * quarter * ROWS))
        return 0

    lax.fori_loop(0, batches, map_batch, 0)
    groups = picked // cols
    for c in range(picked):
        place = pick_ref[c] - base
        held = jnp.logical_and(place >= 0, place < stored)
        place = jnp.where(held, place, 0)
        row = jnp.where(held, rank_of[place // ROWS] * ROWS + place % ROWS, 0)
        rows = coefs[pl.ds(row, box_dev, stride=stored), :]
        out_ref[(c % cols) * groups + c // cols] = jnp.where(held, rows, 0.0).astype(BF16)


def leaf_step(cols, bank, pick, slot_box, leaf_factor):
    box_dev, stored, _ = bank.shape
    picked = pick.shape[0]
    boxes = slot_box.shape[0]
    rank2 = leaf_factor.shape[-1]
    return pl.pallas_call(
        functools.partial(leaf_kernel, cols),
        out_shape=(
            jax.ShapeDtypeStruct((picked, box_dev, rank2), BF16),
            jax.ShapeDtypeStruct((boxes, boxes), BF16),
        ),
        in_specs=[
            pl.BlockSpec(memory_space=pltpu.HBM),
            pl.BlockSpec(memory_space=pltpu.HBM),
            pl.BlockSpec(memory_space=pltpu.HBM),
            pl.BlockSpec(memory_space=pltpu.HBM),
        ],
        out_specs=(
            pl.BlockSpec(memory_space=pltpu.VMEM),
            pl.BlockSpec(memory_space=pltpu.VMEM),
        ),
        scratch_shapes=[
            pltpu.SMEM(pick.shape, jnp.int32),
            pltpu.VMEM((1, boxes), jnp.int32),
            pltpu.VMEM(bank.shape, BF16),
            pltpu.VMEM(leaf_factor.shape, BF16),
            pltpu.VMEM(((box_dev + 1) * stored, rank2), F32),
            pltpu.SMEM((stored // ROWS,), jnp.int32),
            pltpu.SMEM((stored // ROWS,), jnp.int32),
            pltpu.SMEM((stored // ROWS,), jnp.int32),
            pltpu.SemaphoreType.DMA((2,)),
            pltpu.SemaphoreType.DMA((box_dev // BATCH, stored // ROWS)),
            pltpu.SemaphoreType.DMA((box_dev // BATCH,)),
        ],
        compiler_params=pltpu.CompilerParams(vmem_limit_bytes=LEAF_VMEM * MIB),
        name="select_and_leaf",
    )(
        pltpu.with_memory_space_constraint(pick, pltpu.HBM),
        pltpu.with_memory_space_constraint(slot_box.reshape(1, boxes), pltpu.HBM),
        pltpu.with_memory_space_constraint(bank, pltpu.HBM),
        pltpu.with_memory_space_constraint(leaf_factor, pltpu.HBM),
    )


def order_kernel(perm_ref, sent_ref, out_ref):
    devices, groups, box_dev, width = sent_ref.shape
    total = sent_ref[:, 0].astype(F32)
    for t in range(1, groups):
        total = total + sent_ref[:, t].astype(F32)
    rows = total.reshape(devices * box_dev, width).astype(BF16)
    out_ref[...] = dot(perm_ref[...], rows).astype(BF16).reshape(out_ref.shape)


def order_step(perm, sent):
    devices, _, box_dev, width = sent.shape
    return pl.pallas_call(
        order_kernel,
        out_shape=jax.ShapeDtypeStruct((devices, box_dev, width), BF16),
        in_specs=[pl.BlockSpec(memory_space=pltpu.VMEM)] * 2,
        out_specs=pl.BlockSpec(memory_space=pltpu.VMEM),
        compiler_params=pltpu.CompilerParams(vmem_limit_bytes=8 * MIB),
        name="leaf_order",
    )(perm, sent)


def local_kernel(local_bits, leaves_ref, self_ref, cross_ref, out_ref, wide, state):
    cols, slots, rank2 = leaves_ref.shape
    rank = rank2 // 2
    wide[: cols * slots, :] = leaves_ref[...].astype(F32).reshape(cols * slots, rank2)
    for s in range(slots):
        state[0, s] = wide[pl.ds(s, cols, stride=slots), :]
    for level in range(local_bits):
        span = 1 << level
        now, later = level % 2, (level + 1) % 2
        for s in range(slots):
            if s & span:
                continue
            p = s | span
            left = jnp.concatenate([self_ref[level, s], cross_ref[level, s]], axis=0)
            right = jnp.concatenate([cross_ref[level, p], self_ref[level, p]], axis=0)
            both = dot(
                stack_pair(state[now, s], state[now, p], rank),
                jnp.concatenate([left, right], axis=1),
            )
            for place, product in ((s, both[:, :rank2]), (p, both[:, rank2:])):
                mixed = combine(product[:cols], product[cols:], rank)
                if level == local_bits - 1:
                    out_ref[place] = mixed.astype(BF16)
                else:
                    state[later, place] = mixed


def local_step(local_bits, leaves, self_factor, cross_factor):
    cols, slots, rank2 = leaves.shape
    return pl.pallas_call(
        functools.partial(local_kernel, local_bits),
        out_shape=jax.ShapeDtypeStruct((slots, cols, rank2), BF16),
        in_specs=[pl.BlockSpec(memory_space=pltpu.VMEM)] * 3,
        out_specs=pl.BlockSpec(memory_space=pltpu.VMEM),
        scratch_shapes=[
            pltpu.VMEM(((cols + 1) * slots, rank2), F32),
            pltpu.VMEM((2, slots, cols, rank2), F32),
        ],
        compiler_params=pltpu.CompilerParams(vmem_limit_bytes=16 * MIB),
        name="local_levels",
    )(leaves, self_factor, cross_factor)


def turn_kernel(level, _, self_ref, cross_ref, out_ref):
    slots, rank, rank2 = out_ref.shape[1:]
    low = lanes_below((rank, rank2), rank)

    def step(s, _):
        for k, factor in enumerate((self_ref, cross_ref)):
            turned = pltpu.roll(factor[level, s].astype(F32), rank, 1)
            out_ref[k, s] = jnp.where(low, -turned, turned).astype(BF16)
        return 0

    lax.fori_loop(0, slots, step, 0, unroll=8)


def turn_step(level, after, self_factor, cross_factor):
    shape = (2,) + self_factor.shape[1:]
    size = 2 * 2 * shape[1] * shape[2] * shape[3]
    return pl.pallas_call(
        functools.partial(turn_kernel, level),
        out_shape=jax.ShapeDtypeStruct(shape, BF16),
        in_specs=[
            pl.BlockSpec(memory_space=pl.ANY),
            pl.BlockSpec(memory_space=pltpu.VMEM),
            pl.BlockSpec(memory_space=pltpu.VMEM),
        ],
        out_specs=pl.BlockSpec(memory_space=pltpu.VMEM),
        cost_estimate=pl.CostEstimate(flops=size, bytes_accessed=2 * size, transcendentals=0),
        compiler_params=pltpu.CompilerParams(vmem_limit_bytes=12 * MIB),
        name="turn_factors",
    )(after, self_factor, cross_factor)


def mix_pair(level, offset, i, own_ref, other_ref, self_ref, cross_ref, turned_ref):
    cols, rank2 = own_ref.shape[1:]
    rows, factors = [], []
    for k in (i, i + 1):
        s = offset + k
        rows.append(jnp.concatenate([own_ref[k], other_ref[k]], axis=1))
        factors.append(
            jnp.concatenate(
                [self_ref[level, s], turned_ref[0, s], cross_ref[level, s], turned_ref[1, s]], axis=0
            )
        )
    both = dot(jnp.concatenate(rows, axis=0), jnp.concatenate(factors, axis=1))
    return both[:cols, :rank2], both[cols:, rank2:]


def pair_kernel(level, own_ref, other_ref, self_ref, cross_ref, turned_ref, *out_refs):
    size = out_refs[0].shape[0]
    for i in range(0, own_ref.shape[0], 2):
        pair = mix_pair(level, 0, i, own_ref, other_ref, self_ref, cross_ref, turned_ref)
        for k in range(2):
            out_refs[(i + k) // size][(i + k) % size] = pair[k].astype(BF16)


def pair_step(level, parts, own, other, self_factor, cross_factor, turned):
    shape = (own.shape[0] // parts,) + own.shape[1:]
    return pl.pallas_call(
        functools.partial(pair_kernel, level),
        out_shape=(jax.ShapeDtypeStruct(shape, BF16),) * parts,
        in_specs=[pl.BlockSpec(memory_space=pltpu.VMEM)] * 5,
        out_specs=(pl.BlockSpec(memory_space=pltpu.VMEM),) * parts,
        compiler_params=pltpu.CompilerParams(vmem_limit_bytes=16 * MIB),
        name="pair_level",
    )(own, other, self_factor, cross_factor, turned)


GROUP = 4
TILE = 512


def field_kernel(
    level,
    offset,
    own_ref,
    other_ref,
    self_ref,
    cross_ref,
    turned_ref,
    target_ref,
    *rest,
):
    out_ref, final, result, sems = rest[-4:]
    slots, cols, rank2 = own_ref.shape
    rank = rank2 // 2
    points = target_ref.shape[-1] // 2
    for i in range(0, slots, 2):
        pair = mix_pair(level, offset, i, own_ref, other_ref, self_ref, cross_ref, turned_ref)
        final[i] = pair[0]
        final[i + 1] = pair[1]

    def out_copy(q):
        part = pl.ds(q * GROUP, GROUP)
        there = pl.ds(offset + q * GROUP, GROUP)
        return pltpu.make_async_copy(result.at[part], out_ref.at[there], sems.at[q])

    def group(q):
        rows = []
        for i in range(GROUP):
            values = final[q * GROUP + i]
            turned = pltpu.roll(values, rank, 1)
            low = lanes_below(values.shape, rank)
            real, imag = (values, turned) if i % 2 == 0 else (turned, values)
            keep = low if i % 2 == 0 else jnp.logical_not(low)
            block = jnp.concatenate([jnp.where(keep, real, 0.0), jnp.where(keep, imag, 0.0)], axis=0)
            empty = jnp.zeros_like(block)
            rows.append(
                jnp.concatenate([block if j == i // 2 else empty for j in range(GROUP // 2)], axis=1)
            )
        rows = jnp.concatenate(rows, axis=0).astype(BF16)
        part = pl.ds(offset + q * GROUP, GROUP)
        for start in range(0, points, TILE):
            real_part = target_ref[part, :, pl.ds(start, TILE)].reshape(GROUP * rank, TILE)
            imag_part = target_ref[part, :, pl.ds(points + start, TILE)].reshape(GROUP * rank, TILE)
            by_real = dot(rows, real_part)
            by_imag = dot(rows, imag_part)
            for i in range(GROUP):
                xr = slice(2 * cols * i, 2 * cols * i + cols)
                xi = slice(2 * cols * i + cols, 2 * cols * (i + 1))
                box = q * GROUP + i
                result[box, :, pl.ds(start, TILE)] = (by_real[xr] - by_imag[xi]).astype(BF16)
                result[box, :, pl.ds(points + start, TILE)] = (by_imag[xr] + by_real[xi]).astype(BF16)
        out_copy(q).start()

    for q in range(slots // GROUP):
        group(q)
    for q in range(slots // GROUP):
        out_copy(q).wait()


def field_step(level, offset, own, other, self_factor, cross_factor, turned, target, filled):
    slots, cols, rank2 = own.shape
    width = target.shape[-1]
    in_specs = [pl.BlockSpec(memory_space=pltpu.VMEM)] * 6
    operands = [own, other, self_factor, cross_factor, turned]
    operands.append(pltpu.with_memory_space_constraint(target, pltpu.VMEM))
    aliases = {}
    if filled is not None:
        in_specs.append(pl.BlockSpec(memory_space=pl.ANY))
        operands.append(filled)
        aliases = {6: 0}
    return pl.pallas_call(
        functools.partial(field_kernel, level, offset),
        out_shape=jax.ShapeDtypeStruct((target.shape[0], cols, width), BF16),
        in_specs=in_specs,
        out_specs=pl.BlockSpec(memory_space=pl.ANY),
        scratch_shapes=[
            pltpu.VMEM((slots, cols, rank2), F32),
            pltpu.VMEM((slots, cols, width), BF16),
            pltpu.SemaphoreType.DMA((slots // GROUP,)),
        ],
        input_output_aliases=aliases,
        compiler_params=pltpu.CompilerParams(vmem_limit_bytes=20 * MIB),
        name="last_level_and_field",
    )(*operands)


def per_device(bank, pick, slot_box, leaf_factor, self_factor, cross_factor, target_factor):
    box_dev = bank.shape[0]
    devices = lax.axis_size("box")
    groups = lax.axis_size("tx")
    cols = pick.shape[0] // groups
    rank2 = leaf_factor.shape[-1]
    levels = self_factor.shape[0]
    local_bits = box_dev.bit_length() - 1
    parts = devices // cols
    width = rank2 // parts

    sent, perm = leaf_step(cols, bank, pick, slot_box, leaf_factor)
    if parts > 1:
        sent = sent.reshape(cols, groups, box_dev, parts, width).transpose(0, 3, 1, 2, 4)
        sent = sent.reshape(devices * groups, box_dev, width)
    sent = lax.all_to_all(sent, ("box", "tx"), 0, 0, tiled=True)
    ordered = order_step(perm, sent.reshape(devices, groups, box_dev, width))
    leaves = lax.all_to_all(ordered, "box", 0, 0, tiled=True)
    if parts > 1:
        leaves = leaves.reshape(cols, parts, box_dev, width).transpose(0, 2, 1, 3)
        leaves = leaves.reshape(cols, box_dev, rank2)
    current = (local_step(local_bits, leaves, self_factor, cross_factor),)
    for level in range(local_bits, levels):
        bit = 1 << (level - local_bits)
        route = [(i, i ^ bit) for i in range(devices)]
        turned = turn_step(level, current[0], self_factor, cross_factor)
        others = [lax.ppermute(part, "box", route) for part in current]
        if level < levels - 1:
            parts = LAST_PARTS if level == levels - 2 else 1
            current = pair_step(
                level, parts, *current, *others, self_factor, cross_factor, turned
            )
    field, offset = None, 0
    for own, other in zip(current, others, strict=True):
        field = field_step(
            level, offset, own, other, self_factor, cross_factor, turned, target_factor, field
        )
        offset += own.shape[0]
    return field


def solution(mesh):
    in_specs = (
        P("box", "tx", None),
        P(),
        P(),
        P("box", None, None),
        P(None, "box", None, None),
        P(None, "box", None, None),
        P("box", None, None),
    )
    out_specs = P("box", "tx", None)
    return jax.shard_map(
        per_device, mesh=mesh, in_specs=in_specs, out_specs=out_specs, check_vma=False
    )
```

```python
import functools

import jax
import jax.numpy as jnp
from jax import lax
from jax.experimental import pallas as pl
from jax.experimental.pallas import tpu as pltpu
from jax.sharding import PartitionSpec as P

BF16 = jnp.bfloat16
F32 = jnp.float32
MIB = 1 << 20
BATCH = 8
ROWS = 16
LEAF_VMEM = 48
LAST_PARTS = 1


def dot(a, b):
    return jnp.dot(a, b, preferred_element_type=F32)


def lanes_below(shape, bound):
    return lax.broadcasted_iota(jnp.int32, shape, len(shape) - 1) < bound


def combine(first, second, rank):
    turned = pltpu.roll(second, rank, 1)
    return first + jnp.where(lanes_below(turned.shape, rank), -turned, turned)


def stack_pair(own, other, rank):
    low = lanes_below(own.shape, rank)
    real = jnp.where(low, own, pltpu.roll(other, rank, 1))
    imag = jnp.where(low, pltpu.roll(own, rank, 1), other)
    return jnp.concatenate([real, imag], axis=0).astype(BF16)


def leaf_kernel(
    cols,
    pick_hbm,
    slot_hbm,
    bank_ref,
    leaf_ref,
    out_ref,
    perm_ref,
    pick_ref,
    slot_ref,
    bank,
    leaf,
    chooser,
    chosen,
    coefs,
    present,
    wanted,
    rank_of,
    index_sems,
    bank_sems,
    leaf_sems,
):
    box_dev, stored, width = bank_ref.shape
    unknowns = width // 2
    rank = leaf_ref.shape[-1] // 2
    picked = pick_ref.shape[0]
    base = lax.axis_index("tx") * stored
    row_groups = stored // ROWS
    few = row_groups * 3 // 4
    batches = box_dev // BATCH

    def leaf_copy(g):
        part = pl.ds(g * BATCH, BATCH)
        return pltpu.make_async_copy(leaf_ref.at[part], leaf.at[part], leaf_sems.at[g])

    def bank_copy(g, j):
        part = pl.ds(g * BATCH, BATCH)
        source = pl.ds(pl.multiple_of(wanted[j] * ROWS, ROWS), ROWS)
        target = pl.ds(pl.multiple_of(j * ROWS, ROWS), ROWS)
        return pltpu.make_async_copy(
            bank_ref.at[part, source], bank.at[part, target], bank_sems.at[g, j]
        )

    pick_copy = pltpu.make_async_copy(pick_hbm, pick_ref, index_sems.at[0])
    slot_copy = pltpu.make_async_copy(slot_hbm, slot_ref, index_sems.at[1])
    pick_copy.start()
    slot_copy.start()
    for g in range(2):
        leaf_copy(g).start()
    pick_copy.wait()
    for k in range(row_groups):
        present[k] = 0
    for c in range(picked):
        place = pick_ref[c] - base

        @pl.when(jnp.logical_and(place >= 0, place < stored))
        def _():
            present[place // ROWS] = 1

    count = jnp.int32(0)
    for k in range(row_groups):
        wanted[count] = k
        rank_of[k] = count
        count = count + present[k]

    for g in range(batches):
        lax.fori_loop(0, count, lambda j, _, g=g: (bank_copy(g, j).start(), 0)[1], 0)
        if g > 1:
            leaf_copy(g).start()

    row = lax.broadcasted_iota(jnp.int32, (picked, stored), 0)
    column = lax.broadcasted_iota(jnp.int32, (picked, stored), 1)
    target = jnp.full((picked, stored), -1, jnp.int32)
    for c in range(picked):
        place = pick_ref[c] - base
        held = jnp.logical_and(place >= 0, place < stored)
        place = jnp.where(held, place, 0)
        place = jnp.where(held, rank_of[place // ROWS] * ROWS + place % ROWS, -1)
        target = jnp.where(row == c, place, target)
    chooser[...] = (target == column).astype(F32).astype(BF16)

    def blank(j, _):
        rows = pl.ds(pl.multiple_of(j * ROWS, ROWS), ROWS)
        for b in range(box_dev):
            bank[b, rows, :] = jnp.zeros((ROWS, width), BF16)
        return 0

    lax.fori_loop(count, jnp.where(count <= few, few, row_groups), blank, 0)

    slot_copy.wait()
    boxes = slot_ref.shape[1]
    for c in range(0, boxes, 128):
        box = lax.broadcasted_iota(jnp.int32, (boxes, 128), 0)
        hit = (box == slot_ref[:, c : c + 128]).astype(F32)
        perm_ref[c : c + 128, :] = hit.T.astype(BF16)

    def select(g, rows):
        for b in range(g * BATCH, (g + 1) * BATCH):
            values = dot(chooser[:, :rows], bank[b, :rows, :]).astype(BF16)
            chosen[b % (2 * BATCH)] = jnp.concatenate(
                [values[:, :unknowns], values[:, unknowns:]], axis=0
            )

    def map_boxes(g):
        for b in range(g * BATCH, (g + 1) * BATCH):
            product = dot(chosen[b % (2 * BATCH)], leaf[b])
            coefs[b * picked : (b + 1) * picked, :] = combine(
                product[:picked], product[picked:], rank
            )

    def advance(g, rows):
        select(g, rows)
        if g > 0:
            map_boxes(g - 1)

    for g in range(batches):
        if g > 0:
            leaf_copy(g - 1).wait()
        lax.fori_loop(0, count, lambda j, _, g=g: (bank_copy(g, j).wait(), 0)[1], 0)
        pl.when(count <= few)(functools.partial(advance, g, few * ROWS))
        pl.when(count > few)(functools.partial(advance, g, stored))
    leaf_copy(batches - 1).wait()
    map_boxes(batches - 1)
    groups = picked // cols
    for c in range(picked):
        rows = coefs[pl.ds(c, box_dev, stride=picked), :]
        out_ref[(c % cols) * groups + c // cols] = rows.astype(BF16)


def leaf_step(cols, bank, pick, slot_box, leaf_factor):
    box_dev, stored, width = bank.shape
    picked = pick.shape[0]
    boxes = slot_box.shape[0]
    steps = box_dev // BATCH
    rank2 = leaf_factor.shape[-1]
    return pl.pallas_call(
        functools.partial(leaf_kernel, cols),
        out_shape=(
            jax.ShapeDtypeStruct((picked, box_dev, rank2), BF16),
            jax.ShapeDtypeStruct((boxes, boxes), BF16),
        ),
        in_specs=[pl.BlockSpec(memory_space=pltpu.HBM)] * 4,
        out_specs=(
            pl.BlockSpec(memory_space=pltpu.VMEM),
            pl.BlockSpec(memory_space=pltpu.VMEM),
        ),
        scratch_shapes=[
            pltpu.SMEM(pick.shape, jnp.int32),
            pltpu.VMEM((1, boxes), jnp.int32),
            pltpu.VMEM(bank.shape, BF16),
            pltpu.VMEM(leaf_factor.shape, BF16),
            pltpu.VMEM((picked, stored), BF16),
            pltpu.VMEM((2 * BATCH, 2 * picked, width // 2), BF16),
            pltpu.VMEM(((box_dev + 1) * picked, rank2), F32),
            pltpu.SMEM((stored // ROWS,), jnp.int32),
            pltpu.SMEM((stored // ROWS,), jnp.int32),
            pltpu.SMEM((stored // ROWS,), jnp.int32),
            pltpu.SemaphoreType.DMA((2,)),
            pltpu.SemaphoreType.DMA((steps, stored // ROWS)),
            pltpu.SemaphoreType.DMA((steps,)),
        ],
        compiler_params=pltpu.CompilerParams(vmem_limit_bytes=LEAF_VMEM * MIB),
        name="select_and_leaf",
    )(
        *(
            pltpu.with_memory_space_constraint(array, pltpu.HBM)
            for array in (pick, slot_box.reshape(1, boxes), bank, leaf_factor)
        )
    )


def order_kernel(perm_ref, sent_ref, out_ref):
    devices, groups, box_dev, width = sent_ref.shape
    total = sent_ref[:, 0].astype(F32)
    for t in range(1, groups):
        total = total + sent_ref[:, t].astype(F32)
    rows = total.reshape(devices * box_dev, width).astype(BF16)
    out_ref[...] = dot(perm_ref[...], rows).astype(BF16).reshape(out_ref.shape)


def order_step(perm, sent):
    devices, _, box_dev, width = sent.shape
    return pl.pallas_call(
        order_kernel,
        out_shape=jax.ShapeDtypeStruct((devices, box_dev, width), BF16),
        in_specs=[pl.BlockSpec(memory_space=pltpu.VMEM)] * 2,
        out_specs=pl.BlockSpec(memory_space=pltpu.VMEM),
        compiler_params=pltpu.CompilerParams(vmem_limit_bytes=8 * MIB),
        name="leaf_order",
    )(perm, sent)


def local_kernel(local_bits, leaves_ref, self_ref, cross_ref, out_ref, wide, state):
    cols, slots, rank2 = leaves_ref.shape
    rank = rank2 // 2
    wide[: cols * slots, :] = leaves_ref[...].astype(F32).reshape(cols * slots, rank2)
    for s in range(slots):
        state[0, s] = wide[pl.ds(s, cols, stride=slots), :]
    for level in range(local_bits):
        span = 1 << level
        now, later = level % 2, (level + 1) % 2
        for s in range(slots):
            if s & span:
                continue
            p = s | span
            left = jnp.concatenate([self_ref[level, s], cross_ref[level, s]], axis=0)
            right = jnp.concatenate([cross_ref[level, p], self_ref[level, p]], axis=0)
            both = dot(
                stack_pair(state[now, s], state[now, p], rank),
                jnp.concatenate([left, right], axis=1),
            )
            for place, product in ((s, both[:, :rank2]), (p, both[:, rank2:])):
                mixed = combine(product[:cols], product[cols:], rank)
                if level == local_bits - 1:
                    out_ref[place] = mixed.astype(BF16)
                else:
                    state[later, place] = mixed


def local_step(local_bits, leaves, self_factor, cross_factor):
    cols, slots, rank2 = leaves.shape
    return pl.pallas_call(
        functools.partial(local_kernel, local_bits),
        out_shape=jax.ShapeDtypeStruct((slots, cols, rank2), BF16),
        in_specs=[pl.BlockSpec(memory_space=pltpu.VMEM)] * 3,
        out_specs=pl.BlockSpec(memory_space=pltpu.VMEM),
        scratch_shapes=[
            pltpu.VMEM(((cols + 1) * slots, rank2), F32),
            pltpu.VMEM((2, slots, cols, rank2), F32),
        ],
        compiler_params=pltpu.CompilerParams(vmem_limit_bytes=16 * MIB),
        name="local_levels",
    )(leaves, self_factor, cross_factor)


def turn_kernel(level, _, self_ref, cross_ref, out_ref):
    slots, rank, rank2 = out_ref.shape[1:]
    low = lanes_below((rank, rank2), rank)

    def step(s, _):
        for k, factor in enumerate((self_ref, cross_ref)):
            turned = pltpu.roll(factor[level, s].astype(F32), rank, 1)
            out_ref[k, s] = jnp.where(low, -turned, turned).astype(BF16)
        return 0

    lax.fori_loop(0, slots, step, 0, unroll=8)


def turn_step(level, after, self_factor, cross_factor):
    shape = (2,) + self_factor.shape[1:]
    size = 2 * 2 * shape[1] * shape[2] * shape[3]
    return pl.pallas_call(
        functools.partial(turn_kernel, level),
        out_shape=jax.ShapeDtypeStruct(shape, BF16),
        in_specs=[
            pl.BlockSpec(memory_space=pl.ANY),
            pl.BlockSpec(memory_space=pltpu.VMEM),
            pl.BlockSpec(memory_space=pltpu.VMEM),
        ],
        out_specs=pl.BlockSpec(memory_space=pltpu.VMEM),
        cost_estimate=pl.CostEstimate(flops=size, bytes_accessed=2 * size, transcendentals=0),
        compiler_params=pltpu.CompilerParams(vmem_limit_bytes=12 * MIB),
        name="turn_factors",
    )(after, self_factor, cross_factor)


def mix_pair(level, offset, i, own_ref, other_ref, self_ref, cross_ref, turned_ref):
    cols, rank2 = own_ref.shape[1:]
    rows, factors = [], []
    for k in (i, i + 1):
        s = offset + k
        rows.append(jnp.concatenate([own_ref[k], other_ref[k]], axis=1))
        factors.append(
            jnp.concatenate(
                [self_ref[level, s], turned_ref[0, s], cross_ref[level, s], turned_ref[1, s]], axis=0
            )
        )
    both = dot(jnp.concatenate(rows, axis=0), jnp.concatenate(factors, axis=1))
    return both[:cols, :rank2], both[cols:, rank2:]


def pair_kernel(level, own_ref, other_ref, self_ref, cross_ref, turned_ref, *out_refs):
    size = out_refs[0].shape[0]
    for i in range(0, own_ref.shape[0], 2):
        pair = mix_pair(level, 0, i, own_ref, other_ref, self_ref, cross_ref, turned_ref)
        for k in range(2):
            out_refs[(i + k) // size][(i + k) % size] = pair[k].astype(BF16)


def pair_step(level, parts, own, other, self_factor, cross_factor, turned):
    shape = (own.shape[0] // parts,) + own.shape[1:]
    return pl.pallas_call(
        functools.partial(pair_kernel, level),
        out_shape=(jax.ShapeDtypeStruct(shape, BF16),) * parts,
        in_specs=[pl.BlockSpec(memory_space=pltpu.VMEM)] * 5,
        out_specs=(pl.BlockSpec(memory_space=pltpu.VMEM),) * parts,
        compiler_params=pltpu.CompilerParams(vmem_limit_bytes=16 * MIB),
        name="pair_level",
    )(own, other, self_factor, cross_factor, turned)


GROUP = 4
TILE = 512


def field_kernel(
    level,
    offset,
    own_ref,
    other_ref,
    self_ref,
    cross_ref,
    turned_ref,
    target_ref,
    *rest,
):
    out_ref, final, result, sems = rest[-4:]
    slots, cols, rank2 = own_ref.shape
    rank = rank2 // 2
    points = target_ref.shape[-1] // 2
    for i in range(0, slots, 2):
        pair = mix_pair(level, offset, i, own_ref, other_ref, self_ref, cross_ref, turned_ref)
        final[i] = pair[0]
        final[i + 1] = pair[1]

    def out_copy(q):
        part = pl.ds(q * GROUP, GROUP)
        there = pl.ds(offset + q * GROUP, GROUP)
        return pltpu.make_async_copy(result.at[part], out_ref.at[there], sems.at[q])

    def group(q):
        rows = []
        for i in range(GROUP):
            values = final[q * GROUP + i]
            turned = pltpu.roll(values, rank, 1)
            low = lanes_below(values.shape, rank)
            real, imag = (values, turned) if i % 2 == 0 else (turned, values)
            keep = low if i % 2 == 0 else jnp.logical_not(low)
            block = jnp.concatenate([jnp.where(keep, real, 0.0), jnp.where(keep, imag, 0.0)], axis=0)
            empty = jnp.zeros_like(block)
            rows.append(
                jnp.concatenate([block if j == i // 2 else empty for j in range(GROUP // 2)], axis=1)
            )
        rows = jnp.concatenate(rows, axis=0).astype(BF16)
        part = pl.ds(offset + q * GROUP, GROUP)
        for start in range(0, points, TILE):
            real_part = target_ref[part, :, pl.ds(start, TILE)].reshape(GROUP * rank, TILE)
            imag_part = target_ref[part, :, pl.ds(points + start, TILE)].reshape(GROUP * rank, TILE)
            by_real = dot(rows, real_part)
            by_imag = dot(rows, imag_part)
            for i in range(GROUP):
                xr = slice(2 * cols * i, 2 * cols * i + cols)
                xi = slice(2 * cols * i + cols, 2 * cols * (i + 1))
                box = q * GROUP + i
                result[box, :, pl.ds(start, TILE)] = (by_real[xr] - by_imag[xi]).astype(BF16)
                result[box, :, pl.ds(points + start, TILE)] = (by_imag[xr] + by_real[xi]).astype(BF16)
        out_copy(q).start()

    for q in range(slots // GROUP):
        group(q)
    for q in range(slots // GROUP):
        out_copy(q).wait()


def field_step(level, offset, own, other, self_factor, cross_factor, turned, target, filled):
    slots, cols, rank2 = own.shape
    width = target.shape[-1]
    in_specs = [pl.BlockSpec(memory_space=pltpu.VMEM)] * 6
    operands = [own, other, self_factor, cross_factor, turned]
    operands.append(pltpu.with_memory_space_constraint(target, pltpu.VMEM))
    aliases = {}
    if filled is not None:
        in_specs.append(pl.BlockSpec(memory_space=pl.ANY))
        operands.append(filled)
        aliases = {6: 0}
    return pl.pallas_call(
        functools.partial(field_kernel, level, offset),
        out_shape=jax.ShapeDtypeStruct((target.shape[0], cols, width), BF16),
        in_specs=in_specs,
        out_specs=pl.BlockSpec(memory_space=pl.ANY),
        scratch_shapes=[
            pltpu.VMEM((slots, cols, rank2), F32),
            pltpu.VMEM((slots, cols, width), BF16),
            pltpu.SemaphoreType.DMA((slots // GROUP,)),
        ],
        input_output_aliases=aliases,
        compiler_params=pltpu.CompilerParams(vmem_limit_bytes=20 * MIB),
        name="last_level_and_field",
    )(*operands)


def per_device(bank, pick, slot_box, leaf_factor, self_factor, cross_factor, target_factor):
    box_dev = bank.shape[0]
    devices = lax.axis_size("box")
    groups = lax.axis_size("tx")
    cols = pick.shape[0] // groups
    rank2 = leaf_factor.shape[-1]
    levels = self_factor.shape[0]
    local_bits = box_dev.bit_length() - 1
    parts = devices // cols
    width = rank2 // parts

    sent, perm = leaf_step(cols, bank, pick, slot_box, leaf_factor)
    if parts > 1:
        sent = sent.reshape(cols, groups, box_dev, parts, width).transpose(0, 3, 1, 2, 4)
        sent = sent.reshape(devices * groups, box_dev, width)
    sent = lax.all_to_all(sent, ("box", "tx"), 0, 0, tiled=True)
    ordered = order_step(perm, sent.reshape(devices, groups, box_dev, width))
    leaves = lax.all_to_all(ordered, "box", 0, 0, tiled=True)
    if parts > 1:
        leaves = leaves.reshape(cols, parts, box_dev, width).transpose(0, 2, 1, 3)
        leaves = leaves.reshape(cols, box_dev, rank2)
    current = (local_step(local_bits, leaves, self_factor, cross_factor),)
    for level in range(local_bits, levels):
        bit = 1 << (level - local_bits)
        route = [(i, i ^ bit) for i in range(devices)]
        turned = turn_step(level, current[0], self_factor, cross_factor)
        others = [lax.ppermute(part, "box", route) for part in current]
        if level < levels - 1:
            parts = LAST_PARTS if level == levels - 2 else 1
            current = pair_step(
                level, parts, *current, *others, self_factor, cross_factor, turned
            )
    field, offset = None, 0
    for own, other in zip(current, others, strict=True):
        field = field_step(
            level, offset, own, other, self_factor, cross_factor, turned, target_factor, field
        )
        offset += own.shape[0]
    return field


def solution(mesh):
    in_specs = (
        P("box", "tx", None),
        P(),
        P(),
        P("box", None, None),
        P(None, "box", None, None),
        P(None, "box", None, None),
        P("box", None, None),
    )
    out_specs = P("box", "tx", None)
    return jax.shard_map(
        per_device, mesh=mesh, in_specs=in_specs, out_specs=out_specs, check_vma=False
    )
```

```python
import functools

import jax
import jax.numpy as jnp
from jax import lax
from jax.experimental import pallas as pl
from jax.experimental.pallas import tpu as pltpu
from jax.sharding import PartitionSpec as P

BF16 = jnp.bfloat16
F32 = jnp.float32
MIB = 1 << 20
BATCH = 8
ROWS = 16
LEAF_VMEM = 48
LAST_PARTS = 1


def dot(a, b):
    return jnp.dot(a, b, preferred_element_type=F32)


def lanes_below(shape, bound):
    return lax.broadcasted_iota(jnp.int32, shape, len(shape) - 1) < bound


def combine(first, second, rank):
    turned = pltpu.roll(second, rank, 1)
    return first + jnp.where(lanes_below(turned.shape, rank), -turned, turned)


def stack_pair(own, other, rank):
    low = lanes_below(own.shape, rank)
    real = jnp.where(low, own, pltpu.roll(other, rank, 1))
    imag = jnp.where(low, pltpu.roll(own, rank, 1), other)
    return jnp.concatenate([real, imag], axis=0).astype(BF16)


def leaf_kernel(
    cols,
    pick_hbm,
    slot_hbm,
    bank_ref,
    leaf_ref,
    out_ref,
    perm_ref,
    pick_ref,
    slot_ref,
    bank,
    leaf,
    chooser,
    chosen,
    coefs,
    present,
    wanted,
    rank_of,
    index_sems,
    bank_sems,
    leaf_sems,
):
    box_dev, stored, width = bank_ref.shape
    unknowns = width // 2
    rank = leaf_ref.shape[-1] // 2
    picked = pick_ref.shape[0]
    base = lax.axis_index("tx") * stored
    row_groups = stored // ROWS
    few = row_groups * 3 // 4
    batches = box_dev // BATCH

    def leaf_copy(g):
        part = pl.ds(g * BATCH, BATCH)
        return pltpu.make_async_copy(leaf_ref.at[part], leaf.at[part], leaf_sems.at[g])

    def bank_copy(g, j):
        part = pl.ds(g * BATCH, BATCH)
        source = pl.ds(pl.multiple_of(wanted[j] * ROWS, ROWS), ROWS)
        target = pl.ds(pl.multiple_of(j * ROWS, ROWS), ROWS)
        return pltpu.make_async_copy(
            bank_ref.at[part, source], bank.at[part, target], bank_sems.at[g, j]
        )

    pick_copy = pltpu.make_async_copy(pick_hbm, pick_ref, index_sems.at[0])
    slot_copy = pltpu.make_async_copy(slot_hbm, slot_ref, index_sems.at[1])
    pick_copy.start()
    slot_copy.start()
    for g in range(2):
        leaf_copy(g).start(priority=1)
    pick_copy.wait()
    for k in range(row_groups):
        present[k] = 0
    for c in range(picked):
        place = pick_ref[c] - base

        @pl.when(jnp.logical_and(place >= 0, place < stored))
        def _():
            present[place // ROWS] = 1

    count = jnp.int32(0)
    for k in range(row_groups):
        wanted[count] = k
        rank_of[k] = count
        count = count + present[k]

    for g in range(batches):
        lax.fori_loop(0, count, lambda j, _, g=g: (bank_copy(g, j).start(), 0)[1], 0)
        if g > 1:
            leaf_copy(g).start(priority=1)

    row = lax.broadcasted_iota(jnp.int32, (picked, stored), 0)
    column = lax.broadcasted_iota(jnp.int32, (picked, stored), 1)
    target = jnp.full((picked, stored), -1, jnp.int32)
    for c in range(picked):
        place = pick_ref[c] - base
        held = jnp.logical_and(place >= 0, place < stored)
        place = jnp.where(held, place, 0)
        place = jnp.where(held, rank_of[place // ROWS] * ROWS + place % ROWS, -1)
        target = jnp.where(row == c, place, target)
    chooser[...] = (target == column).astype(F32).astype(BF16)

    def blank(j, _):
        rows = pl.ds(pl.multiple_of(j * ROWS, ROWS), ROWS)
        for b in range(box_dev):
            bank[b, rows, :] = jnp.zeros((ROWS, width), BF16)
        return 0

    lax.fori_loop(count, jnp.where(count <= few, few, row_groups), blank, 0)

    slot_copy.wait()
    boxes = slot_ref.shape[1]
    for c in range(0, boxes, 128):
        box = lax.broadcasted_iota(jnp.int32, (boxes, 128), 0)
        hit = (box == slot_ref[:, c : c + 128]).astype(F32)
        perm_ref[c : c + 128, :] = hit.T.astype(BF16)

    def select(g, rows):
        for b in range(g * BATCH, (g + 1) * BATCH):
            values = dot(chooser[:, :rows], bank[b, :rows, :]).astype(BF16)
            chosen[b % (2 * BATCH)] = jnp.concatenate(
                [values[:, :unknowns], values[:, unknowns:]], axis=0
            )

    def map_boxes(g):
        for b in range(g * BATCH, (g + 1) * BATCH):
            product = dot(chosen[b % (2 * BATCH)], leaf[b])
            coefs[b * picked : (b + 1) * picked, :] = combine(
                product[:picked], product[picked:], rank
            )

    def advance(g, rows):
        select(g, rows)
        if g > 0:
            map_boxes(g - 1)

    for g in range(batches):
        if g > 0:
            leaf_copy(g - 1).wait()
        lax.fori_loop(0, count, lambda j, _, g=g: (bank_copy(g, j).wait(), 0)[1], 0)
        pl.when(count <= few)(functools.partial(advance, g, few * ROWS))
        pl.when(count > few)(functools.partial(advance, g, stored))
    leaf_copy(batches - 1).wait()
    map_boxes(batches - 1)
    groups = picked // cols
    for c in range(picked):
        rows = coefs[pl.ds(c, box_dev, stride=picked), :]
        out_ref[(c % cols) * groups + c // cols] = rows.astype(BF16)


def leaf_step(cols, bank, pick, slot_box, leaf_factor):
    box_dev, stored, width = bank.shape
    picked = pick.shape[0]
    boxes = slot_box.shape[0]
    steps = box_dev // BATCH
    rank2 = leaf_factor.shape[-1]
    return pl.pallas_call(
        functools.partial(leaf_kernel, cols),
        out_shape=(
            jax.ShapeDtypeStruct((picked, box_dev, rank2), BF16),
            jax.ShapeDtypeStruct((boxes, boxes), BF16),
        ),
        in_specs=[pl.BlockSpec(memory_space=pltpu.HBM)] * 4,
        out_specs=(
            pl.BlockSpec(memory_space=pltpu.VMEM),
            pl.BlockSpec(memory_space=pltpu.VMEM),
        ),
        scratch_shapes=[
            pltpu.SMEM(pick.shape, jnp.int32),
            pltpu.VMEM((1, boxes), jnp.int32),
            pltpu.VMEM(bank.shape, BF16),
            pltpu.VMEM(leaf_factor.shape, BF16),
            pltpu.VMEM((picked, stored), BF16),
            pltpu.VMEM((2 * BATCH, 2 * picked, width // 2), BF16),
            pltpu.VMEM(((box_dev + 1) * picked, rank2), F32),
            pltpu.SMEM((stored // ROWS,), jnp.int32),
            pltpu.SMEM((stored // ROWS,), jnp.int32),
            pltpu.SMEM((stored // ROWS,), jnp.int32),
            pltpu.SemaphoreType.DMA((2,)),
            pltpu.SemaphoreType.DMA((steps, stored // ROWS)),
            pltpu.SemaphoreType.DMA((steps,)),
        ],
        compiler_params=pltpu.CompilerParams(vmem_limit_bytes=LEAF_VMEM * MIB),
        name="select_and_leaf",
    )(
        *(
            pltpu.with_memory_space_constraint(array, pltpu.HBM)
            for array in (pick, slot_box.reshape(1, boxes), bank, leaf_factor)
        )
    )


def order_kernel(perm_ref, sent_ref, out_ref):
    devices, groups, box_dev, width = sent_ref.shape
    total = sent_ref[:, 0].astype(F32)
    for t in range(1, groups):
        total = total + sent_ref[:, t].astype(F32)
    rows = total.reshape(devices * box_dev, width).astype(BF16)
    out_ref[...] = dot(perm_ref[...], rows).astype(BF16).reshape(out_ref.shape)


def order_step(perm, sent):
    devices, _, box_dev, width = sent.shape
    return pl.pallas_call(
        order_kernel,
        out_shape=jax.ShapeDtypeStruct((devices, box_dev, width), BF16),
        in_specs=[pl.BlockSpec(memory_space=pltpu.VMEM)] * 2,
        out_specs=pl.BlockSpec(memory_space=pltpu.VMEM),
        compiler_params=pltpu.CompilerParams(vmem_limit_bytes=8 * MIB),
        name="leaf_order",
    )(perm, sent)


def local_kernel(local_bits, leaves_ref, self_ref, cross_ref, out_ref, wide, state):
    cols, slots, rank2 = leaves_ref.shape
    rank = rank2 // 2
    wide[: cols * slots, :] = leaves_ref[...].astype(F32).reshape(cols * slots, rank2)
    for s in range(slots):
        state[0, s] = wide[pl.ds(s, cols, stride=slots), :]
    for level in range(local_bits):
        span = 1 << level
        now, later = level % 2, (level + 1) % 2
        for s in range(slots):
            if s & span:
                continue
            p = s | span
            left = jnp.concatenate([self_ref[level, s], cross_ref[level, s]], axis=0)
            right = jnp.concatenate([cross_ref[level, p], self_ref[level, p]], axis=0)
            both = dot(
                stack_pair(state[now, s], state[now, p], rank),
                jnp.concatenate([left, right], axis=1),
            )
            for place, product in ((s, both[:, :rank2]), (p, both[:, rank2:])):
                mixed = combine(product[:cols], product[cols:], rank)
                if level == local_bits - 1:
                    out_ref[place] = mixed.astype(BF16)
                else:
                    state[later, place] = mixed


def local_step(local_bits, leaves, self_factor, cross_factor):
    cols, slots, rank2 = leaves.shape
    return pl.pallas_call(
        functools.partial(local_kernel, local_bits),
        out_shape=jax.ShapeDtypeStruct((slots, cols, rank2), BF16),
        in_specs=[pl.BlockSpec(memory_space=pltpu.VMEM)] * 3,
        out_specs=pl.BlockSpec(memory_space=pltpu.VMEM),
        scratch_shapes=[
            pltpu.VMEM(((cols + 1) * slots, rank2), F32),
            pltpu.VMEM((2, slots, cols, rank2), F32),
        ],
        compiler_params=pltpu.CompilerParams(vmem_limit_bytes=16 * MIB),
        name="local_levels",
    )(leaves, self_factor, cross_factor)


def turn_kernel(level, _, self_ref, cross_ref, out_ref):
    slots, rank, rank2 = out_ref.shape[1:]
    low = lanes_below((rank, rank2), rank)

    def step(s, _):
        for k, factor in enumerate((self_ref, cross_ref)):
            turned = pltpu.roll(factor[level, s].astype(F32), rank, 1)
            out_ref[k, s] = jnp.where(low, -turned, turned).astype(BF16)
        return 0

    lax.fori_loop(0, slots, step, 0, unroll=8)


def turn_step(level, after, self_factor, cross_factor):
    shape = (2,) + self_factor.shape[1:]
    size = 2 * 2 * shape[1] * shape[2] * shape[3]
    return pl.pallas_call(
        functools.partial(turn_kernel, level),
        out_shape=jax.ShapeDtypeStruct(shape, BF16),
        in_specs=[
            pl.BlockSpec(memory_space=pl.ANY),
            pl.BlockSpec(memory_space=pltpu.VMEM),
            pl.BlockSpec(memory_space=pltpu.VMEM),
        ],
        out_specs=pl.BlockSpec(memory_space=pltpu.VMEM),
        cost_estimate=pl.CostEstimate(flops=size, bytes_accessed=2 * size, transcendentals=0),
        compiler_params=pltpu.CompilerParams(vmem_limit_bytes=12 * MIB),
        name="turn_factors",
    )(after, self_factor, cross_factor)


def mix_pair(level, offset, i, own_ref, other_ref, self_ref, cross_ref, turned_ref):
    cols, rank2 = own_ref.shape[1:]
    rows, factors = [], []
    for k in (i, i + 1):
        s = offset + k
        rows.append(jnp.concatenate([own_ref[k], other_ref[k]], axis=1))
        factors.append(
            jnp.concatenate(
                [self_ref[level, s], turned_ref[0, s], cross_ref[level, s], turned_ref[1, s]], axis=0
            )
        )
    both = dot(jnp.concatenate(rows, axis=0), jnp.concatenate(factors, axis=1))
    return both[:cols, :rank2], both[cols:, rank2:]


def pair_kernel(level, own_ref, other_ref, self_ref, cross_ref, turned_ref, *out_refs):
    size = out_refs[0].shape[0]
    for i in range(0, own_ref.shape[0], 2):
        pair = mix_pair(level, 0, i, own_ref, other_ref, self_ref, cross_ref, turned_ref)
        for k in range(2):
            out_refs[(i + k) // size][(i + k) % size] = pair[k].astype(BF16)


def pair_step(level, parts, own, other, self_factor, cross_factor, turned):
    shape = (own.shape[0] // parts,) + own.shape[1:]
    return pl.pallas_call(
        functools.partial(pair_kernel, level),
        out_shape=(jax.ShapeDtypeStruct(shape, BF16),) * parts,
        in_specs=[pl.BlockSpec(memory_space=pltpu.VMEM)] * 5,
        out_specs=(pl.BlockSpec(memory_space=pltpu.VMEM),) * parts,
        compiler_params=pltpu.CompilerParams(vmem_limit_bytes=16 * MIB),
        name="pair_level",
    )(own, other, self_factor, cross_factor, turned)


GROUP = 2
TILE = 2048


def field_kernel(
    level,
    offset,
    own_ref,
    other_ref,
    self_ref,
    cross_ref,
    turned_ref,
    target_ref,
    *rest,
):
    out_ref, final, result, sems = rest[-4:]
    slots, cols, rank2 = own_ref.shape
    rank = rank2 // 2
    points = target_ref.shape[-1] // 2
    tile = min(TILE, points)
    for i in range(0, slots, 2):
        pair = mix_pair(level, offset, i, own_ref, other_ref, self_ref, cross_ref, turned_ref)
        final[i] = pair[0]
        final[i + 1] = pair[1]

    def out_copy(q):
        part = pl.ds(q * GROUP, GROUP)
        there = pl.ds(offset + q * GROUP, GROUP)
        return pltpu.make_async_copy(result.at[part], out_ref.at[there], sems.at[q])

    def group(q):
        rows = []
        for i in range(GROUP):
            values = final[q * GROUP + i]
            turned = pltpu.roll(values, rank, 1)
            low = lanes_below(values.shape, rank)
            real, imag = (values, turned) if i % 2 == 0 else (turned, values)
            keep = low if i % 2 == 0 else jnp.logical_not(low)
            block = jnp.concatenate([jnp.where(keep, real, 0.0), jnp.where(keep, imag, 0.0)], axis=0)
            empty = jnp.zeros_like(block)
            rows.append(
                jnp.concatenate([block if j == i // 2 else empty for j in range(GROUP // 2)], axis=1)
            )
        rows = jnp.concatenate(rows, axis=0).astype(BF16)
        part = pl.ds(offset + q * GROUP, GROUP)
        for start in range(0, points, tile):
            real_part = target_ref[part, :, pl.ds(start, tile)].reshape(GROUP * rank, tile)
            imag_part = target_ref[part, :, pl.ds(points + start, tile)].reshape(GROUP * rank, tile)
            by_real = dot(rows, real_part)
            by_imag = dot(rows, imag_part)
            for i in range(GROUP):
                xr = slice(2 * cols * i, 2 * cols * i + cols)
                xi = slice(2 * cols * i + cols, 2 * cols * (i + 1))
                box = q * GROUP + i
                result[box, :, pl.ds(start, tile)] = (by_real[xr] - by_imag[xi]).astype(BF16)
                result[box, :, pl.ds(points + start, tile)] = (by_imag[xr] + by_real[xi]).astype(BF16)
        out_copy(q).start()

    for q in range(slots // GROUP):
        group(q)
    for q in range(slots // GROUP):
        out_copy(q).wait()


def field_step(level, offset, own, other, self_factor, cross_factor, turned, target, filled):
    slots, cols, rank2 = own.shape
    width = target.shape[-1]
    in_specs = [pl.BlockSpec(memory_space=pltpu.VMEM)] * 6
    operands = [own, other, self_factor, cross_factor, turned]
    operands.append(pltpu.with_memory_space_constraint(target, pltpu.VMEM))
    aliases = {}
    if filled is not None:
        in_specs.append(pl.BlockSpec(memory_space=pl.ANY))
        operands.append(filled)
        aliases = {6: 0}
    return pl.pallas_call(
        functools.partial(field_kernel, level, offset),
        out_shape=jax.ShapeDtypeStruct((target.shape[0], cols, width), BF16),
        in_specs=in_specs,
        out_specs=pl.BlockSpec(memory_space=pl.ANY),
        scratch_shapes=[
            pltpu.VMEM((slots, cols, rank2), F32),
            pltpu.VMEM((slots, cols, width), BF16),
            pltpu.SemaphoreType.DMA((slots // GROUP,)),
        ],
        input_output_aliases=aliases,
        compiler_params=pltpu.CompilerParams(vmem_limit_bytes=20 * MIB),
        name="last_level_and_field",
    )(*operands)


def per_device(bank, pick, slot_box, leaf_factor, self_factor, cross_factor, target_factor):
    box_dev = bank.shape[0]
    devices = lax.axis_size("box")
    groups = lax.axis_size("tx")
    cols = pick.shape[0] // groups
    rank2 = leaf_factor.shape[-1]
    levels = self_factor.shape[0]
    local_bits = box_dev.bit_length() - 1
    parts = devices // cols
    width = rank2 // parts

    sent, perm = leaf_step(cols, bank, pick, slot_box, leaf_factor)
    if parts > 1:
        sent = sent.reshape(cols, groups, box_dev, parts, width).transpose(0, 3, 1, 2, 4)
        sent = sent.reshape(devices * groups, box_dev, width)
    sent = lax.all_to_all(sent, ("box", "tx"), 0, 0, tiled=True)
    ordered = order_step(perm, sent.reshape(devices, groups, box_dev, width))
    leaves = lax.all_to_all(ordered, "box", 0, 0, tiled=True)
    if parts > 1:
        leaves = leaves.reshape(cols, parts, box_dev, width).transpose(0, 2, 1, 3)
        leaves = leaves.reshape(cols, box_dev, rank2)
    current = (local_step(local_bits, leaves, self_factor, cross_factor),)
    for level in range(local_bits, levels):
        bit = 1 << (level - local_bits)
        route = [(i, i ^ bit) for i in range(devices)]
        turned = turn_step(level, current[0], self_factor, cross_factor)
        others = [lax.ppermute(part, "box", route) for part in current]
        if level < levels - 1:
            parts = LAST_PARTS if level == levels - 2 else 1
            current = pair_step(
                level, parts, *current, *others, self_factor, cross_factor, turned
            )
    field, offset = None, 0
    for own, other in zip(current, others, strict=True):
        field = field_step(
            level, offset, own, other, self_factor, cross_factor, turned, target_factor, field
        )
        offset += own.shape[0]
    return field


def solution(mesh):
    in_specs = (
        P("box", "tx", None),
        P(),
        P(),
        P("box", None, None),
        P(None, "box", None, None),
        P(None, "box", None, None),
        P("box", None, None),
    )
    out_specs = P("box", "tx", None)
    return jax.shard_map(
        per_device, mesh=mesh, in_specs=in_specs, out_specs=out_specs, check_vma=False
    )
```
